32 devices in a mesh: dp: 4 (over y, core), slab: 8 (over z, x).
Axes of the slice: x: 2, y: 2, z: 4, core: 2. Of those that a mesh axis runs over, the one named last changes fastest.
Arguments:
- u_field: bfloat16 [4, 128, 32, 128, 128], P('dp', 'slab'), may hold values from -6 to 6
- preact: bfloat16 [4, 128, 32, 128, 128], P('dp', 'slab'), may hold values from -6 to 6
- cotangent: bfloat16 [4, 128, 32, 128, 128], P('dp', 'slab'), may hold values from -6 to 6
- weights: bfloat16 [16, 256, 2048], P(None, 'slab'), may hold values from -6 to 6
Outputs:
- grad_weights: float32 [16, 256, 2048], P('dp', 'slab')
- grad_field: bfloat16 [4, 128, 32, 128, 128], P('dp', 'slab')
The draws below stay inside these ranges and needn't reach their ends.
All inputs are finite; a program needn't handle non-finite values.
Results may differ from the reference program's by a relative error of at most 0.0055.
Values sent between devices are 32-bit elements; how exact they have to be, the bound alone decides.
A program may use at most 192 MiB of HBM per device.

```python
import math
import jax
import jax.numpy as jnp
from jax import lax

C = 32
NX = 128
NY = 128
NZ = 128
MX = 16
MY = 16
MZ = 16
KYZ = 256
SAMPLES = 4


def steps_of(key, extent, cuts, smallest, top_value):
    factor_of, own = 1.0, jax.random.fold_in(key, 6)
    for axis_at, blocks in cuts:
        steps = jnp.exp(jax.random.uniform(jax.random.fold_in(own, axis_at), (blocks,), jnp.float32, smallest / len(cuts), top_value / len(cuts)))
        factor_of = factor_of * jnp.repeat(steps, extent[axis_at] // blocks).reshape([-1 if axis == axis_at else 1 for axis in range(len(extent))])
    return factor_of


def scatter_about(rng, extent, scale, limit, cuts=(), held_as=jnp.bfloat16):
    entries = scale * jax.random.normal(rng, extent, jnp.float32)
    if cuts:
        entries = entries * steps_of(rng, extent, cuts, -0.22, 0.18)
    return jnp.clip(entries, -limit, limit).astype(held_as)


def setup_inputs(seed: int = 0) -> dict:
    key_of = jax.random.split(jax.random.key(seed), 5)
    u_field = scatter_about(key_of[0], (SAMPLES, NX, C, NY, NZ), 1.0, 6.0, ((0, 4), (1, 8)))
    preact = scatter_about(key_of[1], (SAMPLES, NX, C, NY, NZ), 1.0, 6.0, ((0, 4), (1, 8)))
    cotangent = scatter_about(key_of[2], (SAMPLES, NX, C, NY, NZ), 1.0, 6.0, ((0, 4), (1, 8)))
    weights = scatter_about(key_of[3], (MX, KYZ, 2 * C * C), 1.0, 6.0, ((1, 8),))
    return dict(u_field=u_field, preact=preact, cotangent=cotangent, weights=weights)


exact_mode = lax.Precision.HIGHEST

def signed_freqs(count):
    index = jnp.arange(count, dtype=jnp.int32)
    return jnp.where(index < count // 2, index, index - count).astype(jnp.int32)

def twiddles(length, freqs):
    product = jnp.arange(length, dtype=jnp.int32)[:, None] * freqs[None, :] % length
    angle = product.astype(jnp.float32) * (2.0 * math.pi / length)
    return (jnp.cos(angle), jnp.sin(angle))

def gelu_slope(pre):
    return 0.5 * (1.0 + lax.erf(pre * (1.0 / math.sqrt(2.0)))) + pre * jnp.exp(-0.5 * pre * pre) * (1.0 / math.sqrt(2.0 * math.pi))

def transform_planes(field, zcos_low, zsin_low, cos_y, sin_y):
    wide = field.astype(jnp.float32)
    plane_real = jnp.einsum('xcyz,zk->xcyk', wide, zcos_low.astype(jnp.float32), precision=exact_mode)
    plane_imag = jnp.einsum('xcyz,zk->xcyk', wide, zsin_low.astype(jnp.float32), precision=exact_mode)
    out_real = jnp.einsum('xcyk,ym->mkxc', plane_real, cos_y, precision=exact_mode) + jnp.einsum('xcyk,ym->mkxc', plane_imag, sin_y, precision=exact_mode)
    out_imag = jnp.einsum('xcyk,ym->mkxc', plane_imag, cos_y, precision=exact_mode) - jnp.einsum('xcyk,ym->mkxc', plane_real, sin_y, precision=exact_mode)
    return (out_real, out_imag)

def transform_rows(part_real, part_imag, cos_x, sin_x):
    out_real = jnp.einsum('mkxc,xn->nmkc', part_real, cos_x, precision=exact_mode) + jnp.einsum('mkxc,xn->nmkc', part_imag, sin_x, precision=exact_mode)
    out_imag = jnp.einsum('mkxc,xn->nmkc', part_imag, cos_x, precision=exact_mode) - jnp.einsum('mkxc,xn->nmkc', part_real, sin_x, precision=exact_mode)
    return (out_real, out_imag)

def reference(u_field, preact, cotangent, weights):
    cos_x, sin_x = twiddles(NX, signed_freqs(MX))
    cos_y, sin_y = twiddles(NY, signed_freqs(MY))
    cos_z, sin_z = twiddles(NZ, jnp.arange(MZ, dtype=jnp.int32))
    zcos_low = cos_z.astype(jnp.bfloat16)
    zsin_low = (-sin_z).astype(jnp.bfloat16)
    mode_scale = (jnp.where(jnp.arange(MZ) == 0, 1.0, 2.0) / (NX * NY * NZ)).astype(jnp.float32)
    split_weights = weights.astype(jnp.float32).reshape(MX, MY, MZ, 2, C, C)
    weight_real = split_weights[:, :, :, 0]
    weight_imag = split_weights[:, :, :, 1]
    grad_real = jnp.zeros((MX, MY, MZ, C, C), jnp.float32)
    grad_imag = jnp.zeros((MX, MY, MZ, C, C), jnp.float32)
    results = []
    for sample in range(SAMPLES):
        slope = gelu_slope(preact[sample].astype(jnp.float32))
        grad_out = (cotangent[sample].astype(jnp.float32) * slope).astype(jnp.bfloat16)
        ub_real, ub_imag = transform_planes(u_field[sample], zcos_low, zsin_low, cos_y, sin_y)
        gb_real, gb_imag = transform_planes(grad_out, zcos_low, zsin_low, cos_y, sin_y)
        gb_real = gb_real * mode_scale[None, :, None, None]
        gb_imag = gb_imag * mode_scale[None, :, None, None]
        u_real, u_imag = transform_rows(ub_real, ub_imag, cos_x, sin_x)
        g_real, g_imag = transform_rows(gb_real, gb_imag, cos_x, sin_x)
        grad_real = grad_real + jnp.einsum('nmki,nmko->nmkio', u_real, g_real, precision=exact_mode) + jnp.einsum('nmki,nmko->nmkio', u_imag, g_imag, precision=exact_mode)
        grad_imag = grad_imag + jnp.einsum('nmki,nmko->nmkio', u_real, g_imag, precision=exact_mode) - jnp.einsum('nmki,nmko->nmkio', u_imag, g_real, precision=exact_mode)
        back_real = jnp.einsum('nmkio,nmko->nmki', weight_real, g_real, precision=exact_mode) + jnp.einsum('nmkio,nmko->nmki', weight_imag, g_imag, precision=exact_mode)
        back_imag = jnp.einsum('nmkio,nmko->nmki', weight_real, g_imag, precision=exact_mode) - jnp.einsum('nmkio,nmko->nmki', weight_imag, g_real, precision=exact_mode)
        rows_real = jnp.einsum('nmkc,xn->mkxc', back_real, cos_x, precision=exact_mode) - jnp.einsum('nmkc,xn->mkxc', back_imag, sin_x, precision=exact_mode)
        rows_imag = jnp.einsum('nmkc,xn->mkxc', back_imag, cos_x, precision=exact_mode) + jnp.einsum('nmkc,xn->mkxc', back_real, sin_x, precision=exact_mode)
        plane_real = jnp.einsum('mkxc,ym->xcyk', rows_real, cos_y, precision=exact_mode) - jnp.einsum('mkxc,ym->xcyk', rows_imag, sin_y, precision=exact_mode)
        plane_imag = jnp.einsum('mkxc,ym->xcyk', rows_imag, cos_y, precision=exact_mode) + jnp.einsum('mkxc,ym->xcyk', rows_real, sin_y, precision=exact_mode)
        field_grad = jnp.einsum('xcyk,zk->xcyz', plane_real, cos_z, precision=exact_mode) - jnp.einsum('xcyk,zk->xcyz', plane_imag, sin_z, precision=exact_mode)
        results.append(field_grad.astype(jnp.bfloat16))
    grad_weights = jnp.stack([grad_real, grad_imag], axis=3).reshape(MX, KYZ, 2 * C * C)
    return (grad_weights, jnp.stack(results))
```

```python
import functools
import math

import jax
import jax.numpy as jnp
import numpy as np
import ml_dtypes
from jax import lax
from jax.experimental import pallas as pl
from jax.experimental.pallas import tpu as pltpu
from jax.sharding import PartitionSpec as P

C = 32
NX = 128
NY = 128
NZ = 128
MX = 16
MY = 16
MZ = 16
BF = ml_dtypes.bfloat16


def tables(length, freqs):
    product = np.arange(length)[:, None] * freqs[None, :] % length
    angle = product * (2.0 * math.pi / length)
    return np.cos(angle).astype(np.float32), np.sin(angle).astype(np.float32)


def signed(count):
    index = np.arange(count)
    return np.where(index < count // 2, index, index - count)


def halves(table):
    high = table.astype(BF)
    low = (table - high.astype(np.float32)).astype(BF)
    return high, low


COS_X, SIN_X = tables(NX, signed(MX))
COS_Y, SIN_Y = tables(NY, signed(MY))
COS_Z, SIN_Z = tables(NZ, np.arange(MZ))


def forward_tables():
    ty = np.concatenate([COS_Y.T, SIN_Y.T], 0)
    ty = np.concatenate(halves(ty), 0)
    zc = COS_Z.astype(BF).astype(np.float32).T
    zs = (-SIN_Z).astype(BF).astype(np.float32).T
    scale = (np.where(np.arange(MZ) == 0, 1.0, 2.0) / (NX * NY * NZ)).astype(np.float32)[:, None]
    zt = np.zeros((2, 2, MZ, 2, 2, NZ), np.float32)
    for field, factor in ((0, 1.0), (1, scale)):
        zt[field, 0, :, 0, field] = zc * factor
        zt[field, 0, :, 1, field] = zs * factor
        zt[field, 1, :, 0, field] = zs * factor
        zt[field, 1, :, 1, field] = -zc * factor
    return ty, zt.reshape(4 * MZ, 4 * NZ).astype(BF)


def inverse_tables():
    zi = np.zeros((2, MZ, 2, NZ), np.float32)
    zi[0, :, 0] = COS_Z.T
    zi[1, :, 0] = -SIN_Z.T
    zi[0, :, 1] = SIN_Z.T
    zi[1, :, 1] = COS_Z.T
    high, low = halves(zi.reshape(2 * MZ, 2 * NZ))
    zi = np.concatenate([high, high, low], 0)
    yl_high, yl_low = halves(np.concatenate([COS_Y, -SIN_Y], 1))
    yl = np.concatenate([yl_high, yl_high, yl_low], 1)
    return zi, yl


def split_f32(value):
    high = value.astype(jnp.bfloat16)
    low = (value - high.astype(jnp.float32)).astype(jnp.bfloat16)
    return high, low


def dot(a, b, dims=((1,), (0,))):
    return lax.dot_general(a, b, (dims, ((), ())), preferred_element_type=jnp.float32)


def gelu_slope(pre):
    return 0.5 * (1.0 + lax.erf(pre * (1.0 / math.sqrt(2.0)))) + pre * jnp.exp(-0.5 * pre * pre) * (
        1.0 / math.sqrt(2.0 * math.pi)
    )


def forward_kernel(planes, group, owned, cos_ref, sin_ref, ty_ref, zt_ref, u_ref, p_ref, g_ref, out_ref, rows, spec, acc):
    step = pl.program_id(0)

    @pl.when(step == 0)
    def _():
        acc[...] = jnp.zeros_like(acc)

    ty = ty_ref[...]
    for g in range(group):

        def channels(at, carry):
            for k in range(4):
                ch = at * 4 + k
                pre = p_ref[0, g, ch].astype(jnp.float32)
                gh = (g_ref[0, g, ch].astype(jnp.float32) * gelu_slope(pre)).astype(jnp.bfloat16)
                both = dot(ty, jnp.concatenate([u_ref[0, g, ch], gh], axis=1))
                both = both[: 2 * MY] + both[2 * MY :]
                for q in range(2):
                    for w in range(2):
                        rows[2 * q + w, pl.ds(ch, MY, stride=C), :] = both[
                            q * MY : (q + 1) * MY, w * NZ : (w + 1) * NZ
                        ]
            return carry

        lax.fori_loop(0, C // 4, channels, 0)
        high, low = split_f32(jnp.concatenate([rows[q] for q in range(4)], axis=1))
        nt = ((1,), (1,))
        spec[g] = dot(zt_ref[...], high, nt) + dot(zt_ref[...], low, nt)

    x0 = lax.axis_index("slab") * planes + step * group

    def modes(a, carry):
        for f in range(2):
            real = slice(f * 2 * MZ, f * 2 * MZ + MZ)
            imag = slice(f * 2 * MZ + MZ, f * 2 * MZ + 2 * MZ)
            sum_r, sum_i = acc[a, real], acc[a, imag]
            for g in range(group):
                c = cos_ref[(x0 + g) * MX + a]
                s = sin_ref[(x0 + g) * MX + a]
                br, bi = spec[g, real], spec[g, imag]
                sum_r = sum_r + (br * c + bi * s)
                sum_i = sum_i + (bi * c - br * s)
            acc[a, real] = sum_r
            acc[a, imag] = sum_i
        return carry

    lax.fori_loop(0, MX, modes, 0)

    @pl.when(step == pl.num_programs(0) - 1)
    def _():
        size = min(MZ, owned)

        def shuffle(a, carry):
            for b in range(MY):
                part = jnp.concatenate(
                    [acc[a, q * MZ : (q + 1) * MZ, b * C : (b + 1) * C] for q in range(4)], axis=1
                )
                for j in range(0, MZ, size):
                    row = b * MZ + j
                    out_ref[row // owned, a, row % owned : row % owned + size] = part[j : j + size]
            return carry

        lax.fori_loop(0, MX, shuffle, 0)


def mode_kernel(owned, x_ref, w_ref, e_ref, out_ref):
    half = owned // 2
    gr = x_ref[:, 2 * C : 3 * C]
    gi = x_ref[:, 3 * C : 4 * C]
    gr = jnp.concatenate([gr] * 4, axis=1)
    gi = jnp.concatenate([gi] * 4, axis=1)
    total = None
    width = C * C
    for k in range(width // 128):
        wr = w_ref[:, k * 128 : (k + 1) * 128].astype(jnp.float32)
        wi = w_ref[:, width + k * 128 : width + (k + 1) * 128].astype(jnp.float32)
        both = jnp.concatenate([wr * gr + wi * gi, wr * gi - wi * gr], axis=1)
        high, low = split_f32(both)
        part = dot(high, e_ref[k]) + dot(low, e_ref[k])
        total = part if total is None else total + part
    for a in range(out_ref.shape[0]):
        mine = total[a * owned : (a + 1) * owned]
        out_ref[a] = jnp.concatenate([mine[:half], mine[half:]], axis=1)


def gradient_kernel(x_ref, e_ref, out_ref):
    samples = x_ref.shape[0]
    width = C * C
    tiled = []
    for s in range(samples):
        high, low = split_f32(x_ref[s, :, : 2 * C])
        gr = jnp.concatenate([x_ref[s, :, 2 * C : 3 * C]] * 4, axis=1)
        gi = jnp.concatenate([x_ref[s, :, 3 * C : 4 * C]] * 4, axis=1)
        tiled.append((high, low, gr, gi))
    for k in range(width // 128):
        real = imag = None
        for high, low, gr, gi in tiled:
            wide = dot(high, e_ref[k]) + dot(low, e_ref[k])
            ur, ui = wide[:, :128], wide[:, 128:]
            r, i = ur * gr + ui * gi, ur * gi - ui * gr
            real = r if real is None else real + r
            imag = i if imag is None else imag + i
        out_ref[:, k * 128 : (k + 1) * 128] = real
        out_ref[:, width + k * 128 : width + (k + 1) * 128] = imag


def inverse_kernel(planes, group, owned, cos_ref, sin_ref, zi_ref, yl_ref, d_ref, out_ref, modes, mid):
    step = pl.program_id(0)
    half = owned // 2

    @pl.when(step == 0)
    def _():
        def unpack(a, carry):
            for s in range(d_ref.shape[0]):
                for h in range(2):
                    row = s * owned + h * half
                    for j in range(0, half, min(half, MZ)):
                        b, c = (row + j) // MZ, (row + j) % MZ
                        size = min(half, MZ)
                        for q in range(2):
                            modes[a, q * MZ + c : q * MZ + c + size, b * C : (b + 1) * C] = d_ref[
                                s, a, j : j + size, h * 2 * C + q * C : h * 2 * C + (q + 1) * C
                            ]
            return carry

        lax.fori_loop(0, MX, unpack, 0)

    x0 = lax.axis_index("slab") * planes + step * group
    yl = yl_ref[...]
    for g in range(group):

        def add(a, carry):
            real, imag = carry
            c = cos_ref[(x0 + g) * MX + a]
            s = sin_ref[(x0 + g) * MX + a]
            ur, ui = modes[a, :MZ], modes[a, MZ:]
            return real + (ur * c - ui * s), imag + (ui * c + ur * s)

        zero = jnp.zeros((MZ, MY * C), jnp.float32)
        real, imag = lax.fori_loop(0, MX, add, (zero, zero))
        high, low = split_f32(jnp.concatenate([real, imag], axis=0))
        both = dot(jnp.concatenate([high, low, high], axis=0), zi_ref[...], ((0,), (0,)))
        mid[0] = both[:, :NZ]
        mid[1] = both[:, NZ:]

        def channels(at, carry):
            for k in range(4):
                ch = at * 8 + 2 * k
                parts = [
                    [
                        mid[q, pl.ds(ch + n, MY, stride=C), :]
                        for n in range(2)
                    ]
                    for q in range(2)
                ]
                wide = jnp.concatenate([jnp.concatenate(p, axis=1) for p in parts], axis=0)
                high, low = split_f32(wide)
                result = dot(yl, jnp.concatenate([high, low, high], axis=0)).astype(jnp.bfloat16)
                out_ref[0, g, ch] = result[:, :NZ]
                out_ref[0, g, ch + 1] = result[:, NZ:]
            return carry

        lax.fori_loop(0, C // 8, channels, 0)


def sum_table():
    e = np.zeros((8, 2, 4, C, 2, C), np.float32)
    for k in range(8):
        for q in range(2):
            for j in range(4):
                e[k, q, j, :, q, 4 * k + j] = 1.0
    return e.reshape(8, 256, 2 * C).astype(BF)


VMEM = pl.BlockSpec(memory_space=pltpu.VMEM)
SMEM = pl.BlockSpec(memory_space=pltpu.SMEM)


def whole(array):
    rank = len(array.shape)
    return pl.BlockSpec(array.shape, lambda i: (0,) * rank)


def body(u_field, preact, cotangent, weights):
    planes = u_field.shape[1]
    slabs = lax.axis_size("slab")
    dps = lax.axis_size("dp")
    owned = MY * MZ // slabs
    group = min(2, planes)
    cos_x, sin_x = jnp.asarray(COS_X.reshape(-1)), jnp.asarray(SIN_X.reshape(-1))
    ty, zt = (jnp.asarray(t) for t in forward_tables())
    zi, yl = (jnp.asarray(t) for t in inverse_tables())
    table = sum_table()
    e_sum = jnp.asarray(table)
    e_wide = jnp.asarray(np.ascontiguousarray(table.transpose(0, 2, 1)))
    field_spec = pl.BlockSpec((1, group, C, NY, NZ), lambda i: (0, i, 0, 0, 0))
    params = pltpu.CompilerParams(vmem_limit_bytes=50 * 2**20)

    partial = pl.pallas_call(
        functools.partial(forward_kernel, planes, group, owned),
        grid=(planes // group,),
        in_specs=[SMEM, SMEM, whole(ty), whole(zt), field_spec, field_spec, field_spec],
        out_specs=pl.BlockSpec((slabs, MX, owned, 4 * C), lambda i: (0, 0, 0, 0)),
        out_shape=jax.ShapeDtypeStruct((slabs, MX, owned, 4 * C), jnp.float32),
        scratch_shapes=[
            pltpu.VMEM((4, MY * C, NZ), jnp.float32),
            pltpu.VMEM((group, 4 * MZ, MY * C), jnp.float32),
            pltpu.VMEM((MX, 4 * MZ, MY * C), jnp.float32),
        ],
        compiler_params=params,
    )(cos_x, sin_x, ty, zt, u_field, preact, cotangent)

    own = lax.psum_scatter(partial, "slab", scatter_dimension=0, tiled=True)[0]
    rows = MX * owned
    cut = 4
    back = pl.pallas_call(
        functools.partial(mode_kernel, owned),
        grid=(cut,),
        in_specs=[
            pl.BlockSpec((rows // cut, 4 * C), lambda i: (i, 0)),
            pl.BlockSpec((rows // cut, 2 * C * C), lambda i: (i, 0)),
            whole(e_sum),
        ],
        out_specs=pl.BlockSpec((MX // cut, owned // 2, 4 * C), lambda i: (i, 0, 0)),
        out_shape=jax.ShapeDtypeStruct((MX, owned // 2, 4 * C), jnp.float32),
        compiler_params=params,
    )(own.reshape(rows, 4 * C), weights.reshape(rows, 2 * C * C), e_sum)
    spread = lax.all_gather(back, "slab", axis=0, tiled=False)

    share = MX // dps
    swapped = lax.all_to_all(
        own.reshape(dps, share, owned, 4 * C), "dp", split_axis=0, concat_axis=0, tiled=True
    ).reshape(dps, share * owned, 4 * C)
    grad_weights = pl.pallas_call(
        gradient_kernel,
        in_specs=[VMEM, VMEM],
        out_specs=VMEM,
        out_shape=jax.ShapeDtypeStruct((share * owned, 2 * C * C), jnp.float32),
        compiler_params=params,
    )(swapped, e_wide).reshape(share, owned, 2 * C * C)

    grad_field = pl.pallas_call(
        functools.partial(inverse_kernel, planes, group, owned),
        grid=(planes // group,),
        in_specs=[SMEM, SMEM, whole(zi), whole(yl), whole(spread)],
        out_specs=field_spec,
        out_shape=jax.ShapeDtypeStruct((1, planes, C, NY, NZ), jnp.bfloat16),
        scratch_shapes=[
            pltpu.VMEM((MX, 2 * MZ, MY * C), jnp.float32),
            pltpu.VMEM((2, MY * C, NZ), jnp.float32),
        ],
        compiler_params=params,
    )(cos_x, sin_x, zi, yl, spread)
    return grad_weights, grad_field


def solution(mesh):
    placed = (
        P("dp", "slab", None, None, None),
        P("dp", "slab", None, None, None),
        P("dp", "slab", None, None, None),
        P(None, "slab", None),
    )
    return jax.shard_map(
        body,
        mesh=mesh,
        in_specs=placed,
        out_specs=(P("dp", "slab", None), P("dp", "slab", None, None, None)),
        check_vma=False,
    )
```

```python
import functools
import math

import jax
import jax.numpy as jnp
import numpy as np
import ml_dtypes
from jax import lax
from jax.experimental import pallas as pl
from jax.experimental.pallas import tpu as pltpu
from jax.sharding import PartitionSpec as P

C = 32
NX = 128
NY = 128
NZ = 128
MX = 16
MY = 16
MZ = 16
BF = ml_dtypes.bfloat16


def tables(length, freqs):
    product = np.arange(length)[:, None] * freqs[None, :] % length
    angle = product * (2.0 * math.pi / length)
    return np.cos(angle).astype(np.float32), np.sin(angle).astype(np.float32)


def signed(count):
    index = np.arange(count)
    return np.where(index < count // 2, index, index - count)


def halves(table):
    high = table.astype(BF)
    low = (table - high.astype(np.float32)).astype(BF)
    return high, low


COS_X, SIN_X = tables(NX, signed(MX))
COS_Y, SIN_Y = tables(NY, signed(MY))
COS_Z, SIN_Z = tables(NZ, np.arange(MZ))


def forward_tables():
    ty = np.concatenate([COS_Y.T, SIN_Y.T], 0)
    ty = np.concatenate(halves(ty), 0)
    zc = COS_Z.astype(BF).astype(np.float32).T
    zs = (-SIN_Z).astype(BF).astype(np.float32).T
    scale = (np.where(np.arange(MZ) == 0, 1.0, 2.0) / (NX * NY * NZ)).astype(np.float32)[:, None]
    zt = np.zeros((2, 2, MZ, 2, 2, NZ), np.float32)
    for field, factor in ((0, 1.0), (1, scale)):
        zt[field, 0, :, 0, field] = zc * factor
        zt[field, 0, :, 1, field] = zs * factor
        zt[field, 1, :, 0, field] = zs * factor
        zt[field, 1, :, 1, field] = -zc * factor
    return ty, zt.reshape(4 * MZ, 4 * NZ).astype(BF)


def inverse_tables():
    zi = np.zeros((2, MZ, 2, NZ), np.float32)
    zi[0, :, 0] = COS_Z.T
    zi[1, :, 0] = -SIN_Z.T
    zi[0, :, 1] = SIN_Z.T
    zi[1, :, 1] = COS_Z.T
    high, low = halves(zi.reshape(2 * MZ, 2 * NZ))
    zi = np.concatenate([high, high, low], 0)
    yl_high, yl_low = halves(np.concatenate([COS_Y, -SIN_Y], 1))
    yl = np.concatenate([yl_high, yl_high, yl_low], 1)
    return zi, yl


def split_f32(value):
    high = value.astype(jnp.bfloat16)
    low = (value - high.astype(jnp.float32)).astype(jnp.bfloat16)
    return high, low


def dot(a, b, dims=((1,), (0,))):
    return lax.dot_general(a, b, (dims, ((), ())), preferred_element_type=jnp.float32)


def gelu_slope(pre):
    return 0.5 * (1.0 + lax.erf(pre * (1.0 / math.sqrt(2.0)))) + pre * jnp.exp(-0.5 * pre * pre) * (
        1.0 / math.sqrt(2.0 * math.pi)
    )


def quarter_turn(value):
    q = [value[..., k * C : (k + 1) * C] for k in range(4)]
    return jnp.concatenate([q[1], -q[0], q[3], -q[2]], axis=-1)


def forward_kernel(planes, group, owned, slabs, cos_ref, sin_ref, ty_ref, zt_ref, u_ref, p_ref, g_ref, out_ref, rows, send, held, send_sem, recv_sem):
    step = pl.program_id(0)
    steps = planes // group
    me = lax.axis_index("slab")

    def peer(k):
        return lax.rem(me + k, slabs)

    def copy(at, k_to, k_from):
        return pltpu.make_async_remote_copy(
            src_ref=send.at[at, k_to],
            dst_ref=held.at[at, k_from],
            send_sem=send_sem.at[at, k_to],
            recv_sem=recv_sem.at[at, k_from],
            device_id=(lax.axis_index("dp"), k_to),
            device_id_type=pl.DeviceIdType.MESH,
        )

    barrier = pltpu.get_barrier_semaphore()

    @pl.when(step == 0)
    def _():
        def greet(k, carry):
            pl.semaphore_signal(
                barrier, inc=1, device_id=(lax.axis_index("dp"), peer(k)), device_id_type=pl.DeviceIdType.MESH
            )
            return carry

        lax.fori_loop(1, slabs, greet, 0)

    ty = ty_ref[...]
    size = min(MZ, owned)
    unroll = 16
    for g in range(group):

        def channels(at, carry):
            for k in range(unroll):
                ch = at * unroll + k
                pre = p_ref[0, g, ch].astype(jnp.float32)
                gh = (g_ref[0, g, ch].astype(jnp.float32) * gelu_slope(pre)).astype(jnp.bfloat16)
                both = dot(ty, jnp.concatenate([u_ref[0, g, ch], gh], axis=1))
                both = both[: 2 * MY] + both[2 * MY :]
                for q in range(2):
                    for w in range(2):
                        rows[2 * q + w, pl.ds(ch, MY, stride=C), :] = both[
                            q * MY : (q + 1) * MY, w * NZ : (w + 1) * NZ
                        ]
            return carry

        lax.fori_loop(0, C // unroll, channels, 0)
        high, low = split_f32(jnp.concatenate([rows[q] for q in range(4)], axis=1))
        nt = ((1,), (1,))
        spec = dot(zt_ref[...], high, nt) + dot(zt_ref[...], low, nt)
        for b in range(MY):
            part = jnp.concatenate(
                [spec[q * MZ : (q + 1) * MZ, b * C : (b + 1) * C] for q in range(4)], axis=1
            )
            for j in range(0, MZ, size):
                row = b * MZ + j
                send[step, row // owned, g, row % owned : row % owned + size] = part[j : j + size]

    @pl.when(step == 0)
    def _():
        pl.semaphore_wait(barrier, slabs - 1)

    def push(k, carry):
        copy(step, peer(k), me).start()
        return carry

    lax.fori_loop(1, slabs, push, 0)
    held[step, me] = send[step, me]

    @pl.when(step == steps - 1)
    def _():
        for at in range(steps):

            def arrive(k, carry):
                copy(at, peer(k), peer(k)).wait_recv()
                return carry

            lax.fori_loop(1, slabs, arrive, 0)

        for low, high in ((0, 5), (5, MX // 2 + 1)):

            def planes_of(src, totals):
                totals = list(totals)
                for at in range(steps):
                    for g in range(group):
                        value = held[at, src, g]
                        x = (src * planes + at * group + g) * MX
                        for n, f in enumerate(range(low, high)):
                            totals[2 * n] = totals[2 * n] + value * cos_ref[x + f]
                            if f:
                                totals[2 * n + 1] = totals[2 * n + 1] + value * sin_ref[x + f]
                return tuple(totals)

            zero = jnp.zeros((owned, 4 * C), jnp.float32)
            totals = lax.fori_loop(0, slabs, planes_of, (zero,) * (2 * (high - low)))
            for n, f in enumerate(range(low, high)):
                turned = quarter_turn(totals[2 * n + 1])
                out_ref[f] = totals[2 * n] + turned
                if 0 < f < MX // 2:
                    out_ref[MX - f] = totals[2 * n] - turned

        for at in range(steps):

            def sent(k, carry):
                copy(at, peer(k), me).wait_send()
                return carry

            lax.fori_loop(1, slabs, sent, 0)


def mode_kernel(owned, x_ref, w_ref, e_ref, out_ref):
    half = owned // 2
    gr = x_ref[:, 2 * C : 3 * C]
    gi = x_ref[:, 3 * C : 4 * C]
    gr = jnp.concatenate([gr] * 4, axis=1)
    gi = jnp.concatenate([gi] * 4, axis=1)
    total = None
    width = C * C
    for k in range(width // 128):
        wr = w_ref[:, k * 128 : (k + 1) * 128].astype(jnp.float32)
        wi = w_ref[:, width + k * 128 : width + (k + 1) * 128].astype(jnp.float32)
        both = jnp.concatenate([wr * gr + wi * gi, wr * gi - wi * gr], axis=1)
        high, low = split_f32(both)
        part = dot(high, e_ref[k]) + dot(low, e_ref[k])
        total = part if total is None else total + part
    for a in range(out_ref.shape[0]):
        mine = total[a * owned : (a + 1) * owned]
        out_ref[a] = jnp.concatenate([mine[:half], mine[half:]], axis=1)


def gradient_kernel(x_ref, e_ref, out_ref):
    samples = x_ref.shape[0]
    width = C * C
    tiled = []
    for s in range(samples):
        high, low = split_f32(x_ref[s, :, : 2 * C])
        gr = jnp.concatenate([x_ref[s, :, 2 * C : 3 * C]] * 4, axis=1)
        gi = jnp.concatenate([x_ref[s, :, 3 * C : 4 * C]] * 4, axis=1)
        tiled.append((high, low, gr, gi))
    for k in range(width // 128):
        real = imag = None
        for high, low, gr, gi in tiled:
            wide = dot(high, e_ref[k]) + dot(low, e_ref[k])
            ur, ui = wide[:, :128], wide[:, 128:]
            r, i = ur * gr + ui * gi, ur * gi - ui * gr
            real = r if real is None else real + r
            imag = i if imag is None else imag + i
        out_ref[:, k * 128 : (k + 1) * 128] = real
        out_ref[:, width + k * 128 : width + (k + 1) * 128] = imag


def inverse_kernel(planes, group, owned, cos_ref, sin_ref, zi_ref, yl_ref, d_ref, out_ref, modes, mid):
    step = pl.program_id(0)
    half = owned // 2

    @pl.when(step == 0)
    def _():
        def unpack(a, carry):
            for s in range(d_ref.shape[0]):
                for h in range(2):
                    row = s * owned + h * half
                    for j in range(0, half, min(half, MZ)):
                        b, c = (row + j) // MZ, (row + j) % MZ
                        size = min(half, MZ)
                        for q in range(2):
                            modes[a, q * MZ + c : q * MZ + c + size, b * C : (b + 1) * C] = d_ref[
                                s, a, j : j + size, h * 2 * C + q * C : h * 2 * C + (q + 1) * C
                            ]
            return carry

        lax.fori_loop(0, MX, unpack, 0)

    x0 = lax.axis_index("slab") * planes + step * group
    yl = yl_ref[...]
    for g in range(group):

        def add(a, carry):
            real, imag = carry
            c = cos_ref[(x0 + g) * MX + a]
            s = sin_ref[(x0 + g) * MX + a]
            ur, ui = modes[a, :MZ], modes[a, MZ:]
            return real + (ur * c - ui * s), imag + (ui * c + ur * s)

        zero = jnp.zeros((MZ, MY * C), jnp.float32)
        real, imag = lax.fori_loop(0, MX, add, (zero, zero))
        high, low = split_f32(jnp.concatenate([real, imag], axis=0))
        both = dot(jnp.concatenate([high, low, high], axis=0), zi_ref[...], ((0,), (0,)))
        mid[0] = both[:, :NZ]
        mid[1] = both[:, NZ:]

        def channels(at, carry):
            for k in range(8):
                ch = at * 16 + 2 * k
                parts = [
                    [
                        mid[q, pl.ds(ch + n, MY, stride=C), :]
                        for n in range(2)
                    ]
                    for q in range(2)
                ]
                wide = jnp.concatenate([jnp.concatenate(p, axis=1) for p in parts], axis=0)
                high, low = split_f32(wide)
                result = dot(yl, jnp.concatenate([high, low, high], axis=0)).astype(jnp.bfloat16)
                out_ref[0, g, ch] = result[:, :NZ]
                out_ref[0, g, ch + 1] = result[:, NZ:]
            return carry

        lax.fori_loop(0, C // 16, channels, 0)


def sum_table():
    e = np.zeros((8, 2, 4, C, 2, C), np.float32)
    for k in range(8):
        for q in range(2):
            for j in range(4):
                e[k, q, j, :, q, 4 * k + j] = 1.0
    return e.reshape(8, 256, 2 * C).astype(BF)


VMEM = pl.BlockSpec(memory_space=pltpu.VMEM)
SMEM = pl.BlockSpec(memory_space=pltpu.SMEM)


def whole(array):
    rank = len(array.shape)
    return pl.BlockSpec(array.shape, lambda i: (0,) * rank)


def body(u_field, preact, cotangent, weights):
    planes = u_field.shape[1]
    slabs = lax.axis_size("slab")
    dps = lax.axis_size("dp")
    owned = MY * MZ // slabs
    group = min(2, planes)
    cos_x, sin_x = jnp.asarray(COS_X.reshape(-1)), jnp.asarray(SIN_X.reshape(-1))
    ty, zt = (jnp.asarray(t) for t in forward_tables())
    zi, yl = (jnp.asarray(t) for t in inverse_tables())
    table = sum_table()
    e_sum = jnp.asarray(table)
    e_wide = jnp.asarray(np.ascontiguousarray(table.transpose(0, 2, 1)))
    field_spec = pl.BlockSpec((1, group, C, NY, NZ), lambda i: (0, i, 0, 0, 0))
    params = pltpu.CompilerParams(vmem_limit_bytes=50 * 2**20)

    steps = planes // group
    own = pl.pallas_call(
        functools.partial(forward_kernel, planes, group, owned, slabs),
        grid=(steps,),
        in_specs=[SMEM, SMEM, whole(ty), whole(zt), field_spec, field_spec, field_spec],
        out_specs=pl.BlockSpec((MX, owned, 4 * C), lambda i: (0, 0, 0)),
        out_shape=jax.ShapeDtypeStruct((MX, owned, 4 * C), jnp.float32),
        scratch_shapes=[
            pltpu.VMEM((4, MY * C, NZ), jnp.float32),
            pltpu.VMEM((steps, slabs, group, owned, 4 * C), jnp.float32),
            pltpu.VMEM((steps, slabs, group, owned, 4 * C), jnp.float32),
            pltpu.SemaphoreType.DMA((steps, slabs)),
            pltpu.SemaphoreType.DMA((steps, slabs)),
        ],
        compiler_params=pltpu.CompilerParams(
            vmem_limit_bytes=50 * 2**20, collective_id=0, has_side_effects=True
        ),
    )(cos_x, sin_x, ty, zt, u_field, preact, cotangent)

    rows = MX * owned
    cut = 4
    back = pl.pallas_call(
        functools.partial(mode_kernel, owned),
        grid=(cut,),
        in_specs=[
            pl.BlockSpec((rows // cut, 4 * C), lambda i: (i, 0)),
            pl.BlockSpec((rows // cut, 2 * C * C), lambda i: (i, 0)),
            whole(e_sum),
        ],
        out_specs=pl.BlockSpec((MX // cut, owned // 2, 4 * C), lambda i: (i, 0, 0)),
        out_shape=jax.ShapeDtypeStruct((MX, owned // 2, 4 * C), jnp.float32),
        compiler_params=params,
    )(own.reshape(rows, 4 * C), weights.reshape(rows, 2 * C * C), e_sum)
    spread = lax.all_gather(back, "slab", axis=0, tiled=False)

    share = MX // dps
    swapped = lax.all_to_all(
        own.reshape(dps, share, owned, 4 * C), "dp", split_axis=0, concat_axis=0, tiled=True
    ).reshape(dps, share * owned, 4 * C)
    grad_weights = pl.pallas_call(
        gradient_kernel,
        in_specs=[VMEM, VMEM],
        out_specs=VMEM,
        out_shape=jax.ShapeDtypeStruct((share * owned, 2 * C * C), jnp.float32),
        compiler_params=params,
    )(swapped, e_wide).reshape(share, owned, 2 * C * C)

    grad_field = pl.pallas_call(
        functools.partial(inverse_kernel, planes, group, owned),
        grid=(planes // group,),
        in_specs=[SMEM, SMEM, whole(zi), whole(yl), whole(spread)],
        out_specs=field_spec,
        out_shape=jax.ShapeDtypeStruct((1, planes, C, NY, NZ), jnp.bfloat16),
        scratch_shapes=[
            pltpu.VMEM((MX, 2 * MZ, MY * C), jnp.float32),
            pltpu.VMEM((2, MY * C, NZ), jnp.float32),
        ],
        compiler_params=params,
    )(cos_x, sin_x, zi, yl, spread)
    return grad_weights, grad_field


def solution(mesh):
    placed = (
        P("dp", "slab", None, None, None),
        P("dp", "slab", None, None, None),
        P("dp", "slab", None, None, None),
        P(None, "slab", None),
    )
    return jax.shard_map(
        body,
        mesh=mesh,
        in_specs=placed,
        out_specs=(P("dp", "slab", None), P("dp", "slab", None, None, None)),
        check_vma=False,
    )
```

```python
import functools
import math

import jax
import jax.numpy as jnp
import numpy as np
import ml_dtypes
from jax import lax
from jax.experimental import pallas as pl
from jax.experimental.pallas import tpu as pltpu
from jax.sharding import PartitionSpec as P

C = 32
NX = 128
NY = 128
NZ = 128
MX = 16
MY = 16
MZ = 16
BF = ml_dtypes.bfloat16


def tables(length, freqs):
    product = np.arange(length)[:, None] * freqs[None, :] % length
    angle = product * (2.0 * math.pi / length)
    return np.cos(angle).astype(np.float32), np.sin(angle).astype(np.float32)


def signed(count):
    index = np.arange(count)
    return np.where(index < count // 2, index, index - count)


def halves(table):
    high = table.astype(BF)
    low = (table - high.astype(np.float32)).astype(BF)
    return high, low


COS_X, SIN_X = tables(NX, signed(MX))
COS_Y, SIN_Y = tables(NY, signed(MY))
COS_Z, SIN_Z = tables(NZ, np.arange(MZ))


def forward_tables():
    ty = np.concatenate([COS_Y.T, SIN_Y.T], 0)
    ty = np.concatenate(halves(ty), 0)
    zc = COS_Z.astype(BF).astype(np.float32).T
    zs = (-SIN_Z).astype(BF).astype(np.float32).T
    scale = (np.where(np.arange(MZ) == 0, 1.0, 2.0) / (NX * NY * NZ)).astype(np.float32)[:, None]
    zt = np.zeros((2, 2, MZ, 2, 2, NZ), np.float32)
    for field, factor in ((0, 1.0), (1, scale)):
        zt[field, 0, :, 0, field] = zc * factor
        zt[field, 0, :, 1, field] = zs * factor
        zt[field, 1, :, 0, field] = zs * factor
        zt[field, 1, :, 1, field] = -zc * factor
    return ty, zt.reshape(4 * MZ, 4 * NZ).astype(BF)


def inverse_tables():
    zi = np.zeros((2, MZ, 2, NZ), np.float32)
    zi[0, :, 0] = COS_Z.T
    zi[1, :, 0] = -SIN_Z.T
    zi[0, :, 1] = SIN_Z.T
    zi[1, :, 1] = COS_Z.T
    high, low = halves(zi.reshape(2 * MZ, 2 * NZ))
    zi = np.concatenate([high, high, low], 0)
    yl_high, yl_low = halves(np.concatenate([COS_Y, -SIN_Y], 1))
    yl = np.concatenate([yl_high, yl_high, yl_low], 1)
    return zi, yl


def split_f32(value):
    high = value.astype(jnp.bfloat16)
    low = (value - high.astype(jnp.float32)).astype(jnp.bfloat16)
    return high, low


def dot(a, b, dims=((1,), (0,))):
    return lax.dot_general(a, b, (dims, ((), ())), preferred_element_type=jnp.float32)


def gelu_slope(pre):
    return 0.5 * (1.0 + lax.erf(pre * (1.0 / math.sqrt(2.0)))) + pre * jnp.exp(-0.5 * pre * pre) * (
        1.0 / math.sqrt(2.0 * math.pi)
    )


def quarter_turn(value):
    q = [value[..., k * C : (k + 1) * C] for k in range(4)]
    return jnp.concatenate([q[1], -q[0], q[3], -q[2]], axis=-1)


def forward_kernel(planes, group, owned, slabs, cos_ref, sin_ref, ty_ref, zt_ref, u_ref, p_ref, g_ref, out_ref, rows, send, held, send_sem, recv_sem):
    step = pl.program_id(0)
    steps = planes // group
    me = lax.axis_index("slab")

    def peer(k):
        return lax.rem(me + k, slabs)

    def copy(at, k_to, k_from):
        return pltpu.make_async_remote_copy(
            src_ref=send.at[at, k_to],
            dst_ref=held.at[at, k_from],
            send_sem=send_sem.at[at, k_to],
            recv_sem=recv_sem.at[at, k_from],
            device_id=(lax.axis_index("dp"), k_to),
            device_id_type=pl.DeviceIdType.MESH,
        )

    barrier = pltpu.get_barrier_semaphore()

    @pl.when(step == 0)
    def _():
        def greet(k, carry):
            pl.semaphore_signal(
                barrier, inc=1, device_id=(lax.axis_index("dp"), peer(k)), device_id_type=pl.DeviceIdType.MESH
            )
            return carry

        lax.fori_loop(1, slabs, greet, 0)

    ty = ty_ref[...]
    size = min(MZ, owned)
    unroll = 16
    for g in range(group):

        def channels(at, carry):
            for k in range(unroll):
                ch = at * unroll + k
                pre = p_ref[0, g, ch].astype(jnp.float32)
                gh = (g_ref[0, g, ch].astype(jnp.float32) * gelu_slope(pre)).astype(jnp.bfloat16)
                both = dot(ty, jnp.concatenate([u_ref[0, g, ch], gh], axis=1))
                both = both[: 2 * MY] + both[2 * MY :]
                for q in range(2):
                    for w in range(2):
                        rows[2 * q + w, pl.ds(ch, MY, stride=C), :] = both[
                            q * MY : (q + 1) * MY, w * NZ : (w + 1) * NZ
                        ]
            return carry

        lax.fori_loop(0, C // unroll, channels, 0)
        high, low = split_f32(jnp.concatenate([rows[q] for q in range(4)], axis=1))
        nt = ((1,), (1,))
        spec = dot(zt_ref[...], high, nt) + dot(zt_ref[...], low, nt)
        for b in range(MY):
            part = jnp.concatenate(
                [spec[q * MZ : (q + 1) * MZ, b * C : (b + 1) * C] for q in range(4)], axis=1
            )
            for j in range(0, MZ, size):
                row = b * MZ + j
                send[step, row // owned, g, row % owned : row % owned + size] = part[j : j + size]

    @pl.when(step == 0)
    def _():
        pl.semaphore_wait(barrier, slabs - 1)

    def push(k, carry):
        copy(step, peer(k), me).start()
        return carry

    lax.fori_loop(1, slabs, push, 0)
    held[step, me] = send[step, me]

    @pl.when(step == steps - 1)
    def _():
        for at in range(steps):

            def arrive(k, carry):
                copy(at, peer(k), peer(k)).wait_recv()
                return carry

            lax.fori_loop(1, slabs, arrive, 0)

        for low, high in ((0, 5), (5, MX // 2 + 1)):

            def planes_of(src, totals):
                totals = list(totals)
                for at in range(steps):
                    for g in range(group):
                        value = held[at, src, g]
                        x = (src * planes + at * group + g) * MX
                        for n, f in enumerate(range(low, high)):
                            totals[2 * n] = totals[2 * n] + value * cos_ref[x + f]
                            if f:
                                totals[2 * n + 1] = totals[2 * n + 1] + value * sin_ref[x + f]
                return tuple(totals)

            zero = jnp.zeros((owned, 4 * C), jnp.float32)
            totals = lax.fori_loop(0, slabs, planes_of, (zero,) * (2 * (high - low)))
            for n, f in enumerate(range(low, high)):
                turned = quarter_turn(totals[2 * n + 1])
                out_ref[f] = totals[2 * n] + turned
                if 0 < f < MX // 2:
                    out_ref[MX - f] = totals[2 * n] - turned

        for at in range(steps):

            def sent(k, carry):
                copy(at, peer(k), me).wait_send()
                return carry

            lax.fori_loop(1, slabs, sent, 0)


def back_products(x_ref, w_ref, e_ref, rows):
    gr = jnp.concatenate([x_ref[rows, 2 * C : 3 * C]] * 4, axis=1)
    gi = jnp.concatenate([x_ref[rows, 3 * C : 4 * C]] * 4, axis=1)
    total = None
    width = C * C
    for k in range(width // 128):
        wr = w_ref[rows, k * 128 : (k + 1) * 128].astype(jnp.float32)
        wi = w_ref[rows, width + k * 128 : width + (k + 1) * 128].astype(jnp.float32)
        both = jnp.concatenate([wr * gr + wi * gi, wr * gi - wi * gr], axis=1)
        high, low = split_f32(both)
        part = dot(high, e_ref[k]) + dot(low, e_ref[k])
        total = part if total is None else total + part
    return total


def middle_kernel(owned, slabs, dps, cut, x_ref, w_ref, e_ref, wide_ref, out_ref, grad_ref, send, held, swapped, send_sem, recv_sem, dp_send, dp_recv):
    half = owned // 2
    me = lax.axis_index("slab")
    my_dp = lax.axis_index("dp")
    share = MX // dps * owned
    part_rows = MX // cut * owned

    def peer(k):
        return lax.rem(me + k, slabs)

    def dp_peer(k):
        return lax.rem(my_dp + k, dps)

    def share_of(d):
        return x_ref.at[pl.ds(pl.multiple_of(d * share, share), share)]

    def gather_copy(at, to, source):
        return pltpu.make_async_remote_copy(
            src_ref=send.at[at],
            dst_ref=held.at[at, source],
            send_sem=send_sem.at[at, to],
            recv_sem=recv_sem.at[at, source],
            device_id=(my_dp, to),
            device_id_type=pl.DeviceIdType.MESH,
        )

    def dp_copy(to, source):
        return pltpu.make_async_remote_copy(
            src_ref=share_of(to),
            dst_ref=swapped.at[source],
            send_sem=dp_send.at[to],
            recv_sem=dp_recv.at[source],
            device_id=(to, me),
            device_id_type=pl.DeviceIdType.MESH,
        )

    barrier = pltpu.get_barrier_semaphore()

    def greet(k, carry):
        pl.semaphore_signal(
            barrier, inc=1, device_id=(my_dp, peer(k)), device_id_type=pl.DeviceIdType.MESH
        )
        return carry

    lax.fori_loop(1, slabs, greet, 0)
    for k in range(1, dps):
        pl.semaphore_signal(
            barrier, inc=1, device_id=(dp_peer(k), me), device_id_type=pl.DeviceIdType.MESH
        )

    for at in range(cut):
        total = back_products(x_ref, w_ref, e_ref, slice(at * part_rows, (at + 1) * part_rows))
        for a in range(MX // cut):
            mine = total[a * owned : (a + 1) * owned]
            send[at, a] = jnp.concatenate([mine[:half], mine[half:]], axis=1)
        if at == 0:
            pl.semaphore_wait(barrier, slabs + dps - 2)

        def push(k, carry):
            gather_copy(at, peer(k), me).start()
            return carry

        lax.fori_loop(1, slabs, push, 0)
        held[at, me] = send[at]
        if at == 0:
            for k in range(1, dps):
                dp_copy(dp_peer(k), my_dp).start()
            swapped[my_dp] = share_of(my_dp)[...]

    for k in range(1, dps):
        dp_copy(dp_peer(k), dp_peer(k)).wait_recv()
    gradient_kernel(swapped, wide_ref, grad_ref)

    for at in range(cut):

        def arrive(k, carry):
            gather_copy(at, peer(k), peer(k)).wait_recv()
            return carry

        lax.fori_loop(1, slabs, arrive, 0)

        def place(source, carry):
            out_ref[source, at * (MX // cut) : (at + 1) * (MX // cut)] = held[at, source]
            return carry

        lax.fori_loop(0, slabs, place, 0)

        def sent(k, carry):
            gather_copy(at, peer(k), me).wait_send()
            return carry

        lax.fori_loop(1, slabs, sent, 0)
    for k in range(1, dps):
        dp_copy(dp_peer(k), my_dp).wait_send()


def gradient_kernel(x_ref, e_ref, out_ref):
    samples = x_ref.shape[0]
    width = C * C
    tiled = []
    for s in range(samples):
        high, low = split_f32(x_ref[s, :, : 2 * C])
        gr = jnp.concatenate([x_ref[s, :, 2 * C : 3 * C]] * 4, axis=1)
        gi = jnp.concatenate([x_ref[s, :, 3 * C : 4 * C]] * 4, axis=1)
        tiled.append((high, low, gr, gi))
    for k in range(width // 128):
        real = imag = None
        for high, low, gr, gi in tiled:
            wide = dot(high, e_ref[k]) + dot(low, e_ref[k])
            ur, ui = wide[:, :128], wide[:, 128:]
            r, i = ur * gr + ui * gi, ur * gi - ui * gr
            real = r if real is None else real + r
            imag = i if imag is None else imag + i
        out_ref[:, k * 128 : (k + 1) * 128] = real
        out_ref[:, width + k * 128 : width + (k + 1) * 128] = imag


def inverse_kernel(planes, group, owned, cos_ref, sin_ref, zi_ref, yl_ref, d_ref, out_ref, modes, mid):
    step = pl.program_id(0)
    half = owned // 2

    @pl.when(step == 0)
    def _():
        def unpack(a, carry):
            for s in range(d_ref.shape[0]):
                for h in range(2):
                    row = s * owned + h * half
                    for j in range(0, half, min(half, MZ)):
                        b, c = (row + j) // MZ, (row + j) % MZ
                        size = min(half, MZ)
                        for q in range(2):
                            modes[a, q * MZ + c : q * MZ + c + size, b * C : (b + 1) * C] = d_ref[
                                s, a, j : j + size, h * 2 * C + q * C : h * 2 * C + (q + 1) * C
                            ]
            return carry

        lax.fori_loop(0, MX, unpack, 0)

    x0 = lax.axis_index("slab") * planes + step * group
    yl = yl_ref[...]
    for g in range(group):

        def add(a, carry):
            real, imag = carry
            c = cos_ref[(x0 + g) * MX + a]
            s = sin_ref[(x0 + g) * MX + a]
            ur, ui = modes[a, :MZ], modes[a, MZ:]
            return real + (ur * c - ui * s), imag + (ui * c + ur * s)

        zero = jnp.zeros((MZ, MY * C), jnp.float32)
        real, imag = lax.fori_loop(0, MX, add, (zero, zero))
        high, low = split_f32(jnp.concatenate([real, imag], axis=0))
        both = dot(jnp.concatenate([high, low, high], axis=0), zi_ref[...], ((0,), (0,)))
        mid[0] = both[:, :NZ]
        mid[1] = both[:, NZ:]

        def channels(at, carry):
            for k in range(8):
                ch = at * 16 + 2 * k
                parts = [
                    [
                        mid[q, pl.ds(ch + n, MY, stride=C), :]
                        for n in range(2)
                    ]
                    for q in range(2)
                ]
                wide = jnp.concatenate([jnp.concatenate(p, axis=1) for p in parts], axis=0)
                high, low = split_f32(wide)
                result = dot(yl, jnp.concatenate([high, low, high], axis=0)).astype(jnp.bfloat16)
                out_ref[0, g, ch] = result[:, :NZ]
                out_ref[0, g, ch + 1] = result[:, NZ:]
            return carry

        lax.fori_loop(0, C // 16, channels, 0)


def sum_table():
    e = np.zeros((8, 2, 4, C, 2, C), np.float32)
    for k in range(8):
        for q in range(2):
            for j in range(4):
                e[k, q, j, :, q, 4 * k + j] = 1.0
    return e.reshape(8, 256, 2 * C).astype(BF)


VMEM = pl.BlockSpec(memory_space=pltpu.VMEM)
SMEM = pl.BlockSpec(memory_space=pltpu.SMEM)


def whole(array):
    rank = len(array.shape)
    return pl.BlockSpec(array.shape, lambda i: (0,) * rank)


def body(u_field, preact, cotangent, weights):
    planes = u_field.shape[1]
    slabs = lax.axis_size("slab")
    dps = lax.axis_size("dp")
    owned = MY * MZ // slabs
    group = min(2, planes)
    cos_x, sin_x = jnp.asarray(COS_X.reshape(-1)), jnp.asarray(SIN_X.reshape(-1))
    ty, zt = (jnp.asarray(t) for t in forward_tables())
    zi, yl = (jnp.asarray(t) for t in inverse_tables())
    table = sum_table()
    e_sum = jnp.asarray(table)
    e_wide = jnp.asarray(np.ascontiguousarray(table.transpose(0, 2, 1)))
    field_spec = pl.BlockSpec((1, group, C, NY, NZ), lambda i: (0, i, 0, 0, 0))
    params = pltpu.CompilerParams(vmem_limit_bytes=50 * 2**20)

    steps = planes // group
    own = pl.pallas_call(
        functools.partial(forward_kernel, planes, group, owned, slabs),
        grid=(steps,),
        in_specs=[SMEM, SMEM, whole(ty), whole(zt), field_spec, field_spec, field_spec],
        out_specs=pl.BlockSpec((MX, owned, 4 * C), lambda i: (0, 0, 0)),
        out_shape=jax.ShapeDtypeStruct((MX, owned, 4 * C), jnp.float32),
        scratch_shapes=[
            pltpu.VMEM((4, MY * C, NZ), jnp.float32),
            pltpu.VMEM((steps, slabs, group, owned, 4 * C), jnp.float32),
            pltpu.VMEM((steps, slabs, group, owned, 4 * C), jnp.float32),
            pltpu.SemaphoreType.DMA((steps, slabs)),
            pltpu.SemaphoreType.DMA((steps, slabs)),
        ],
        compiler_params=pltpu.CompilerParams(
            vmem_limit_bytes=50 * 2**20, collective_id=0, has_side_effects=True
        ),
    )(cos_x, sin_x, ty, zt, u_field, preact, cotangent)

    rows = MX * owned
    cut = 4
    half = owned // 2
    share = MX // dps
    spread, grad_weights = pl.pallas_call(
        functools.partial(middle_kernel, owned, slabs, dps, cut),
        in_specs=[VMEM] * 4,
        out_specs=[VMEM] * 2,
        out_shape=[
            jax.ShapeDtypeStruct((slabs, MX, half, 4 * C), jnp.float32),
            jax.ShapeDtypeStruct((share * owned, 2 * C * C), jnp.float32),
        ],
        scratch_shapes=[
            pltpu.VMEM((cut, MX // cut, half, 4 * C), jnp.float32),
            pltpu.VMEM((cut, slabs, MX // cut, half, 4 * C), jnp.float32),
            pltpu.VMEM((dps, share * owned, 4 * C), jnp.float32),
            pltpu.SemaphoreType.DMA((cut, slabs)),
            pltpu.SemaphoreType.DMA((cut, slabs)),
            pltpu.SemaphoreType.DMA((dps,)),
            pltpu.SemaphoreType.DMA((dps,)),
        ],
        compiler_params=pltpu.CompilerParams(
            vmem_limit_bytes=40 * 2**20, collective_id=1, has_side_effects=True
        ),
    )(own.reshape(rows, 4 * C), weights.reshape(rows, 2 * C * C), e_sum, e_wide)
    grad_weights = grad_weights.reshape(share, owned, 2 * C * C)

    grad_field = pl.pallas_call(
        functools.partial(inverse_kernel, planes, group, owned),
        grid=(planes // group,),
        in_specs=[SMEM, SMEM, whole(zi), whole(yl), whole(spread)],
        out_specs=field_spec,
        out_shape=jax.ShapeDtypeStruct((1, planes, C, NY, NZ), jnp.bfloat16),
        scratch_shapes=[
            pltpu.VMEM((MX, 2 * MZ, MY * C), jnp.float32),
            pltpu.VMEM((2, MY * C, NZ), jnp.float32),
        ],
        compiler_params=params,
    )(cos_x, sin_x, zi, yl, spread)
    return grad_weights, grad_field


def solution(mesh):
    placed = (
        P("dp", "slab", None, None, None),
        P("dp", "slab", None, None, None),
        P("dp", "slab", None, None, None),
        P(None, "slab", None),
    )
    return jax.shard_map(
        body,
        mesh=mesh,
        in_specs=placed,
        out_specs=(P("dp", "slab", None), P("dp", "slab", None, None, None)),
        check_vma=False,
    )
```

```python
import functools
import math

import jax
import jax.numpy as jnp
import numpy as np
import ml_dtypes
from jax import lax
from jax.experimental import pallas as pl
from jax.experimental.pallas import tpu as pltpu
from jax.sharding import PartitionSpec as P

C = 32
NX = 128
NY = 128
NZ = 128
MX = 16
MY = 16
MZ = 16
BF = ml_dtypes.bfloat16


def tables(length, freqs):
    product = np.arange(length)[:, None] * freqs[None, :] % length
    angle = product * (2.0 * math.pi / length)
    return np.cos(angle).astype(np.float32), np.sin(angle).astype(np.float32)


def signed(count):
    index = np.arange(count)
    return np.where(index < count // 2, index, index - count)


def halves(table):
    high = table.astype(BF)
    low = (table - high.astype(np.float32)).astype(BF)
    return high, low


COS_X, SIN_X = tables(NX, signed(MX))
COS_Y, SIN_Y = tables(NY, signed(MY))
COS_Z, SIN_Z = tables(NZ, np.arange(MZ))


def forward_tables():
    ty = np.concatenate([COS_Y.T, SIN_Y.T], 0)
    ty = np.concatenate(halves(ty), 0)
    zc = COS_Z.astype(BF).astype(np.float32).T
    zs = (-SIN_Z).astype(BF).astype(np.float32).T
    scale = (np.where(np.arange(MZ) == 0, 1.0, 2.0) / (NX * NY * NZ)).astype(np.float32)[:, None]
    zt = np.zeros((2, 2, MZ, 2, 2, NZ), np.float32)
    for field, factor in ((0, 1.0), (1, scale)):
        zt[field, 0, :, 0, field] = zc * factor
        zt[field, 0, :, 1, field] = zs * factor
        zt[field, 1, :, 0, field] = zs * factor
        zt[field, 1, :, 1, field] = -zc * factor
    return ty, zt.reshape(4 * MZ, 4 * NZ).astype(BF)


def inverse_tables():
    zi = np.zeros((2, MZ, 2, NZ), np.float32)
    zi[0, :, 0] = COS_Z.T
    zi[1, :, 0] = -SIN_Z.T
    zi[0, :, 1] = SIN_Z.T
    zi[1, :, 1] = COS_Z.T
    high, low = halves(zi.reshape(2 * MZ, 2 * NZ))
    zi = np.concatenate([high, high, low], 0)
    yl_high, yl_low = halves(np.concatenate([COS_Y, -SIN_Y], 1))
    yl = np.concatenate([yl_high, yl_high, yl_low], 1)
    return zi, yl


def split_f32(value):
    high = value.astype(jnp.bfloat16)
    low = (value - high.astype(jnp.float32)).astype(jnp.bfloat16)
    return high, low


def dot(a, b, dims=((1,), (0,))):
    return lax.dot_general(a, b, (dims, ((), ())), preferred_element_type=jnp.float32)


def gelu_slope(pre):
    return 0.5 * (1.0 + lax.erf(pre * (1.0 / math.sqrt(2.0)))) + pre * jnp.exp(-0.5 * pre * pre) * (
        1.0 / math.sqrt(2.0 * math.pi)
    )


def quarter_turn(value):
    q = [value[..., k * C : (k + 1) * C] for k in range(4)]
    return jnp.concatenate([q[1], -q[0], q[3], -q[2]], axis=-1)


def forward_kernel(planes, group, owned, slabs, cos_ref, sin_ref, ty_ref, zt_ref, u_ref, p_ref, g_ref, out_ref, rows, send, held, sums, send_sem, recv_sem):
    step = pl.program_id(0)
    steps = planes // group
    me = lax.axis_index("slab")

    def peer(k):
        return lax.rem(me + k, slabs)

    def copy(at, k_to, k_from):
        return pltpu.make_async_remote_copy(
            src_ref=send.at[at, k_to],
            dst_ref=held.at[at, k_from],
            send_sem=send_sem.at[at, k_to],
            recv_sem=recv_sem.at[at, k_from],
            device_id=(lax.axis_index("dp"), k_to),
            device_id_type=pl.DeviceIdType.MESH,
        )

    barrier = pltpu.get_barrier_semaphore()

    @pl.when(step == 0)
    def _():
        def greet(k, carry):
            pl.semaphore_signal(
                barrier, inc=1, device_id=(lax.axis_index("dp"), peer(k)), device_id_type=pl.DeviceIdType.MESH
            )
            return carry

        lax.fori_loop(1, slabs, greet, 0)

    ty = ty_ref[...]
    size = min(MZ, owned)
    unroll = 16
    for g in range(group):

        def channels(at, carry):
            for k in range(unroll):
                ch = at * unroll + k
                pre = p_ref[0, g, ch].astype(jnp.float32)
                gh = (g_ref[0, g, ch].astype(jnp.float32) * gelu_slope(pre)).astype(jnp.bfloat16)
                both = dot(ty, jnp.concatenate([u_ref[0, g, ch], gh], axis=1))
                both = both[: 2 * MY] + both[2 * MY :]
                for q in range(2):
                    for w in range(2):
                        rows[2 * q + w, pl.ds(ch, MY, stride=C), :] = both[
                            q * MY : (q + 1) * MY, w * NZ : (w + 1) * NZ
                        ]
            return carry

        lax.fori_loop(0, C // unroll, channels, 0)
        high, low = split_f32(jnp.concatenate([rows[q] for q in range(4)], axis=1))
        nt = ((1,), (1,))
        spec = dot(zt_ref[...], high, nt) + dot(zt_ref[...], low, nt)
        for b in range(MY):
            part = jnp.concatenate(
                [spec[q * MZ : (q + 1) * MZ, b * C : (b + 1) * C] for q in range(4)], axis=1
            )
            for j in range(0, MZ, size):
                row = b * MZ + j
                send[step, row // owned, g, row % owned : row % owned + size] = part[j : j + size]

    @pl.when(step == 0)
    def _():
        pl.semaphore_wait(barrier, slabs - 1)

    def push(k, carry):
        copy(step, peer(k), me).start()
        return carry

    lax.fori_loop(1, slabs, push, 0)
    held[step, me] = send[step, me]

    def absorb(at):
        def arrive(k, carry):
            copy(at, peer(k), peer(k)).wait_recv()
            return carry

        lax.fori_loop(1, slabs, arrive, 0)
        for low, high in ((0, 5), (5, MX // 2 + 1)):

            def planes_of(src, totals):
                totals = list(totals)
                for g in range(group):
                    value = held[at, src, g]
                    x = (src * planes + at * group + g) * MX
                    for n, f in enumerate(range(low, high)):
                        totals[2 * n] = totals[2 * n] + value * cos_ref[x + f]
                        if f:
                            totals[2 * n + 1] = totals[2 * n + 1] + value * sin_ref[x + f]
                return tuple(totals)

            start = tuple(sums[n] for n in range(2 * low, 2 * high))
            totals = lax.fori_loop(0, slabs, planes_of, start)
            for n in range(2 * low, 2 * high):
                sums[n] = totals[n - 2 * low]

    @pl.when(step == 0)
    def _():
        sums[...] = jnp.zeros_like(sums)

    @pl.when(step >= 2)
    def _():
        absorb(step - 2)

    @pl.when(step == steps - 1)
    def _():
        for at in range(max(steps - 2, 0), steps):
            absorb(at)
        for f in range(MX // 2 + 1):
            turned = quarter_turn(sums[2 * f + 1])
            out_ref[f] = sums[2 * f] + turned
            if 0 < f < MX // 2:
                out_ref[MX - f] = sums[2 * f] - turned

        for at in range(steps):

            def sent(k, carry):
                copy(at, peer(k), me).wait_send()
                return carry

            lax.fori_loop(1, slabs, sent, 0)


def back_products(x_ref, w_ref, e_ref, rows):
    gr = jnp.concatenate([x_ref[rows, 2 * C : 3 * C]] * 4, axis=1)
    gi = jnp.concatenate([x_ref[rows, 3 * C : 4 * C]] * 4, axis=1)
    total = None
    width = C * C
    for k in range(width // 128):
        wr = w_ref[rows, k * 128 : (k + 1) * 128].astype(jnp.float32)
        wi = w_ref[rows, width + k * 128 : width + (k + 1) * 128].astype(jnp.float32)
        both = jnp.concatenate([wr * gr + wi * gi, wr * gi - wi * gr], axis=1)
        high, low = split_f32(both)
        part = dot(high, e_ref[k]) + dot(low, e_ref[k])
        total = part if total is None else total + part
    return total


def middle_kernel(owned, slabs, dps, cut, x_ref, w_ref, e_ref, wide_ref, out_ref, grad_ref, send, held, swapped, send_sem, recv_sem, dp_send, dp_recv):
    half = owned // 2
    me = lax.axis_index("slab")
    my_dp = lax.axis_index("dp")
    share = MX // dps * owned
    part_rows = MX // cut * owned

    def peer(k):
        return lax.rem(me + k, slabs)

    def dp_peer(k):
        return lax.rem(my_dp + k, dps)

    def share_of(d):
        return x_ref.at[pl.ds(pl.multiple_of(d * share, share), share)]

    def gather_copy(at, to, source):
        return pltpu.make_async_remote_copy(
            src_ref=send.at[at],
            dst_ref=held.at[at, source],
            send_sem=send_sem.at[at, to],
            recv_sem=recv_sem.at[at, source],
            device_id=(my_dp, to),
            device_id_type=pl.DeviceIdType.MESH,
        )

    def dp_copy(to, source):
        return pltpu.make_async_remote_copy(
            src_ref=share_of(to),
            dst_ref=swapped.at[source],
            send_sem=dp_send.at[to],
            recv_sem=dp_recv.at[source],
            device_id=(to, me),
            device_id_type=pl.DeviceIdType.MESH,
        )

    barrier = pltpu.get_barrier_semaphore()

    def greet(k, carry):
        pl.semaphore_signal(
            barrier, inc=1, device_id=(my_dp, peer(k)), device_id_type=pl.DeviceIdType.MESH
        )
        return carry

    lax.fori_loop(1, slabs, greet, 0)
    for k in range(1, dps):
        pl.semaphore_signal(
            barrier, inc=1, device_id=(dp_peer(k), me), device_id_type=pl.DeviceIdType.MESH
        )

    for at in range(cut):
        total = back_products(x_ref, w_ref, e_ref, slice(at * part_rows, (at + 1) * part_rows))
        for a in range(MX // cut):
            mine = total[a * owned : (a + 1) * owned]
            send[at, a] = jnp.concatenate([mine[:half], mine[half:]], axis=1)
        if at == 0:
            pl.semaphore_wait(barrier, slabs + dps - 2)

        def push(k, carry):
            gather_copy(at, peer(k), me).start()
            return carry

        lax.fori_loop(1, slabs, push, 0)
        held[at, me] = send[at]
        if at == 0:
            for k in range(1, dps):
                dp_copy(dp_peer(k), my_dp).start()
            swapped[my_dp] = share_of(my_dp)[...]

    for k in range(1, dps):
        dp_copy(dp_peer(k), dp_peer(k)).wait_recv()
    gradient_kernel(swapped, wide_ref, grad_ref)

    for at in range(cut):

        def arrive(k, carry):
            gather_copy(at, peer(k), peer(k)).wait_recv()
            return carry

        lax.fori_loop(1, slabs, arrive, 0)

        def place(source, carry):
            out_ref[source, at * (MX // cut) : (at + 1) * (MX // cut)] = held[at, source]
            return carry

        lax.fori_loop(0, slabs, place, 0)

        def sent(k, carry):
            gather_copy(at, peer(k), me).wait_send()
            return carry

        lax.fori_loop(1, slabs, sent, 0)
    for k in range(1, dps):
        dp_copy(dp_peer(k), my_dp).wait_send()


def gradient_kernel(x_ref, e_ref, out_ref):
    samples = x_ref.shape[0]
    width = C * C
    tiled = []
    for s in range(samples):
        high, low = split_f32(x_ref[s, :, : 2 * C])
        gr = jnp.concatenate([x_ref[s, :, 2 * C : 3 * C]] * 4, axis=1)
        gi = jnp.concatenate([x_ref[s, :, 3 * C : 4 * C]] * 4, axis=1)
        tiled.append((high, low, gr, gi))
    for k in range(width // 128):
        real = imag = None
        for high, low, gr, gi in tiled:
            wide = dot(high, e_ref[k]) + dot(low, e_ref[k])
            ur, ui = wide[:, :128], wide[:, 128:]
            r, i = ur * gr + ui * gi, ur * gi - ui * gr
            real = r if real is None else real + r
            imag = i if imag is None else imag + i
        out_ref[:, k * 128 : (k + 1) * 128] = real
        out_ref[:, width + k * 128 : width + (k + 1) * 128] = imag


def inverse_kernel(planes, group, owned, cos_ref, sin_ref, zi_ref, yl_ref, d_ref, out_ref, modes, mid):
    step = pl.program_id(0)
    half = owned // 2

    @pl.when(step == 0)
    def _():
        def unpack(a, carry):
            for s in range(d_ref.shape[0]):
                for h in range(2):
                    row = s * owned + h * half
                    for j in range(0, half, min(half, MZ)):
                        b, c = (row + j) // MZ, (row + j) % MZ
                        size = min(half, MZ)
                        for q in range(2):
                            modes[a, q * MZ + c : q * MZ + c + size, b * C : (b + 1) * C] = d_ref[
                                s, a, j : j + size, h * 2 * C + q * C : h * 2 * C + (q + 1) * C
                            ]
            return carry

        lax.fori_loop(0, MX, unpack, 0)

    x0 = lax.axis_index("slab") * planes + step * group
    yl = yl_ref[...]
    for g in range(group):

        def add(a, carry):
            real, imag = carry
            c = cos_ref[(x0 + g) * MX + a]
            s = sin_ref[(x0 + g) * MX + a]
            ur, ui = modes[a, :MZ], modes[a, MZ:]
            return real + (ur * c - ui * s), imag + (ui * c + ur * s)

        zero = jnp.zeros((MZ, MY * C), jnp.float32)
        real, imag = lax.fori_loop(0, MX, add, (zero, zero))
        high, low = split_f32(jnp.concatenate([real, imag], axis=0))
        both = dot(jnp.concatenate([high, low, high], axis=0), zi_ref[...], ((0,), (0,)))
        mid[0] = both[:, :NZ]
        mid[1] = both[:, NZ:]

        def channels(at, carry):
            for k in range(8):
                ch = at * 16 + 2 * k
                parts = [
                    [
                        mid[q, pl.ds(ch + n, MY, stride=C), :]
                        for n in range(2)
                    ]
                    for q in range(2)
                ]
                wide = jnp.concatenate([jnp.concatenate(p, axis=1) for p in parts], axis=0)
                high, low = split_f32(wide)
                result = dot(yl, jnp.concatenate([high, low, high], axis=0)).astype(jnp.bfloat16)
                out_ref[0, g, ch] = result[:, :NZ]
                out_ref[0, g, ch + 1] = result[:, NZ:]
            return carry

        lax.fori_loop(0, C // 16, channels, 0)


def sum_table():
    e = np.zeros((8, 2, 4, C, 2, C), np.float32)
    for k in range(8):
        for q in range(2):
            for j in range(4):
                e[k, q, j, :, q, 4 * k + j] = 1.0
    return e.reshape(8, 256, 2 * C).astype(BF)


VMEM = pl.BlockSpec(memory_space=pltpu.VMEM)
SMEM = pl.BlockSpec(memory_space=pltpu.SMEM)


def whole(array):
    rank = len(array.shape)
    return pl.BlockSpec(array.shape, lambda i: (0,) * rank)


def body(u_field, preact, cotangent, weights):
    planes = u_field.shape[1]
    slabs = lax.axis_size("slab")
    dps = lax.axis_size("dp")
    owned = MY * MZ // slabs
    group = min(2, planes)
    cos_x, sin_x = jnp.asarray(COS_X.reshape(-1)), jnp.asarray(SIN_X.reshape(-1))
    ty, zt = (jnp.asarray(t) for t in forward_tables())
    zi, yl = (jnp.asarray(t) for t in inverse_tables())
    table = sum_table()
    e_sum = jnp.asarray(table)
    e_wide = jnp.asarray(np.ascontiguousarray(table.transpose(0, 2, 1)))
    field_spec = pl.BlockSpec((1, group, C, NY, NZ), lambda i: (0, i, 0, 0, 0))
    params = pltpu.CompilerParams(vmem_limit_bytes=50 * 2**20)

    steps = planes // group
    own = pl.pallas_call(
        functools.partial(forward_kernel, planes, group, owned, slabs),
        grid=(steps,),
        in_specs=[SMEM, SMEM, whole(ty), whole(zt), field_spec, field_spec, field_spec],
        out_specs=pl.BlockSpec((MX, owned, 4 * C), lambda i: (0, 0, 0)),
        out_shape=jax.ShapeDtypeStruct((MX, owned, 4 * C), jnp.float32),
        scratch_shapes=[
            pltpu.VMEM((4, MY * C, NZ), jnp.float32),
            pltpu.VMEM((steps, slabs, group, owned, 4 * C), jnp.float32),
            pltpu.VMEM((steps, slabs, group, owned, 4 * C), jnp.float32),
            pltpu.VMEM((MX + 2, owned, 4 * C), jnp.float32),
            pltpu.SemaphoreType.DMA((steps, slabs)),
            pltpu.SemaphoreType.DMA((steps, slabs)),
        ],
        compiler_params=pltpu.CompilerParams(
            vmem_limit_bytes=50 * 2**20, collective_id=0, has_side_effects=True
        ),
    )(cos_x, sin_x, ty, zt, u_field, preact, cotangent)

    rows = MX * owned
    cut = 4
    half = owned // 2
    share = MX // dps
    spread, grad_weights = pl.pallas_call(
        functools.partial(middle_kernel, owned, slabs, dps, cut),
        in_specs=[VMEM] * 4,
        out_specs=[VMEM] * 2,
        out_shape=[
            jax.ShapeDtypeStruct((slabs, MX, half, 4 * C), jnp.float32),
            jax.ShapeDtypeStruct((share * owned, 2 * C * C), jnp.float32),
        ],
        scratch_shapes=[
            pltpu.VMEM((cut, MX // cut, half, 4 * C), jnp.float32),
            pltpu.VMEM((cut, slabs, MX // cut, half, 4 * C), jnp.float32),
            pltpu.VMEM((dps, share * owned, 4 * C), jnp.float32),
            pltpu.SemaphoreType.DMA((cut, slabs)),
            pltpu.SemaphoreType.DMA((cut, slabs)),
            pltpu.SemaphoreType.DMA((dps,)),
            pltpu.SemaphoreType.DMA((dps,)),
        ],
        compiler_params=pltpu.CompilerParams(
            vmem_limit_bytes=40 * 2**20, collective_id=1, has_side_effects=True
        ),
    )(own.reshape(rows, 4 * C), weights.reshape(rows, 2 * C * C), e_sum, e_wide)
    grad_weights = grad_weights.reshape(share, owned, 2 * C * C)

    grad_field = pl.pallas_call(
        functools.partial(inverse_kernel, planes, group, owned),
        grid=(planes // group,),
        in_specs=[SMEM, SMEM, whole(zi), whole(yl), whole(spread)],
        out_specs=field_spec,
        out_shape=jax.ShapeDtypeStruct((1, planes, C, NY, NZ), jnp.bfloat16),
        scratch_shapes=[
            pltpu.VMEM((MX, 2 * MZ, MY * C), jnp.float32),
            pltpu.VMEM((2, MY * C, NZ), jnp.float32),
        ],
        compiler_params=params,
    )(cos_x, sin_x, zi, yl, spread)
    return grad_weights, grad_field


def solution(mesh):
    placed = (
        P("dp", "slab", None, None, None),
        P("dp", "slab", None, None, None),
        P("dp", "slab", None, None, None),
        P(None, "slab", None),
    )
    return jax.shard_map(
        body,
        mesh=mesh,
        in_specs=placed,
        out_specs=(P("dp", "slab", None), P("dp", "slab", None, None, None)),
        check_vma=False,
    )
```
